32 devices in a mesh: rep: 8 (over y, x, core), exp: 4 (over z).
Axes of the slice: x: 2, y: 2, z: 4, core: 2. Of those that a mesh axis runs over, the one named last changes fastest.
Arguments:
- tokens: bfloat16 [64, 197, 768], P(('rep', 'exp')), may hold values from -6 to 6
- routes: int32 [64, 197, 2], P(('rep', 'exp')), may hold values from 0 to 3, all different within a row; in each aligned block of 394 rows (0 to 393, 394 to 787, ..., all dimensions but the last counted through in order) at most 264 rows name the same one
- cotangent: bfloat16 [64, 197, 768], P(('rep', 'exp')), may hold values from -6 to 6
- attn_gain: bfloat16 [768], P('exp'), may hold values from 0.099609375 to 1.8984375
- attn_shift: bfloat16 [768], P('exp'), may hold values from -3 to 3
- qkv_weight: bfloat16 [768, 2304], P('exp'), may hold values from -0.21875 to 0.21875
- query_bias: bfloat16 [768], P('exp'), may hold values from -3 to 3
- value_bias: bfloat16 [768], P('exp'), may hold values from -3 to 3
- proj_weight: bfloat16 [768, 768], P('exp'), may hold values from -0.875 to 0.875
- proj_bias: bfloat16 [768], P('exp'), may hold values from -3 to 3
- moe_gain: bfloat16 [768], P('exp'), may hold values from 0.099609375 to 1.8984375
- moe_shift: bfloat16 [768], P('exp'), may hold values from -3 to 3
- router_weight: bfloat16 [768, 4], P('exp'), may hold values from -0.21875 to 0.21875
- expert_in: bfloat16 [4, 768, 3072], P('exp'), may hold values from -0.21875 to 0.21875
- expert_in_bias: bfloat16 [4, 3072], P('exp'), may hold values from -3 to 3
- expert_out: bfloat16 [4, 3072, 768], P('exp'), may hold values from -0.4375 to 0.4375
- expert_out_bias: bfloat16 [4, 768], P('exp'), may hold values from -3 to 3
Outputs:
- block_out: bfloat16 [64, 197, 768], P(('rep', 'exp'))
- input_grad: float32 [64, 197, 768], P(('rep', 'exp'))
- grad_attn_gain: float32 [768], P('exp')
- grad_attn_shift: float32 [768], P('exp')
- grad_qkv_weight: float32 [768, 2304], P('exp')
- grad_query_bias: float32 [768], P('exp')
- grad_value_bias: float32 [768], P('exp')
- grad_proj_weight: float32 [768, 768], P('exp')
- grad_proj_bias: float32 [768], P('exp')
- grad_moe_gain: float32 [768], P('exp')
- grad_moe_shift: float32 [768], P('exp')
- grad_router_weight: float32 [768, 4], P('exp')
- grad_expert_in: float32 [4, 768, 3072], P('exp')
- grad_expert_in_bias: float32 [4, 3072], P('exp')
- grad_expert_out: float32 [4, 3072, 768], P('exp')
- grad_expert_out_bias: float32 [4, 768], P('exp')
The draws below stay inside these ranges and needn't reach their ends.
Inputs may be any that keep to these rules, and one draw needn't show every extreme that they name: `routes`: in the rows of one device, no expert is named by more than 264 tokens; the two experts of a token differ.
All inputs are finite; a program needn't handle non-finite values.
Results may differ from the reference program's by a relative error of at most 0.025.
Values may be sent and summed in bfloat16 or wider, within the bound.
A program may use at most 192 MiB of HBM per device.

```python
import math
import jax
import jax.numpy as jnp
import numpy as np
from jax import lax

D = 768
HEADS = 12
HEAD_DIM = 64
FF = 3072
LEN = 197
TOK_DEV = 394
IMAGES = 64
EXPERTS = 4
CAP = 264


def spiked(values, stream_key, source, target, shards_of, factor):
    def block_of(dim):
        return (jnp.arange(values.shape[dim]) // (values.shape[dim] // shards_of)).reshape((-1,) + (1,) * (values.ndim - 1 - dim))

    one_side = jax.random.permutation(stream_key, shards_of)[block_of(target)]
    other_side = (block_of(target) + shards_of // 2) % shards_of
    return jnp.where((block_of(source) == one_side) | (block_of(source) == other_side), factor * values, values)


def block_levels(key, shape, shards, least, top_value):
    level = 1.0
    for axis_at, shards_of in shards:
        steps = jax.random.uniform(jax.random.fold_in(jax.random.fold_in(key, 6), axis_at), (shards_of,), jnp.float32, least / len(shards), top_value / len(shards))
        level = level * jnp.repeat(jnp.exp(steps), shape[axis_at] // shards_of).reshape((-1,) + (1,) * (len(shape) - 1 - axis_at))
    return level


def deal_out(rng, own, number, rows, amount, top, reach, lean):
    sequence = jax.random.permutation(rng, amount)
    heavy_load, usual = portions_of(amount, rows * top, reach, lean, True), portions_of(amount, rows * top, reach, lean, False)
    places = jnp.arange(amount)

    def named(tallies, offset_by):
        used = int((tallies > 0).sum())
        fixed = max(1, used // 4)
        shifted = fixed + (places - fixed + offset_by * (used - fixed)) % max(1, amount - fixed)
        return jnp.zeros((amount,), jnp.int32).at[sequence[jnp.where(places < fixed, places, shifted)]].set(jnp.asarray(tallies, jnp.int32))

    tallies = jnp.where(number % 4 == 0, named(heavy_load, number // 4), named(usual, number - number // 4 - 1))
    mixed = jax.random.permutation(jax.random.fold_in(own, 3), amount)
    donor, taker = mixed[0:amount // 2 * 2:2], mixed[1:amount // 2 * 2:2]
    slack = jnp.minimum(tallies[donor] - 1, reach - tallies[taker]) // 2
    slack = jnp.where((donor == sequence[0]) | (taker == sequence[0]) | (tallies[taker] == 0), 0, jnp.maximum(slack, 0))
    shifted = jax.random.randint(jax.random.fold_in(own, 4), (amount // 2,), 0, 1 << 20) % (slack + 1)
    tallies = tallies.at[donor].add(-shifted).at[taker].add(shifted)
    labels = jnp.searchsorted(jnp.cumsum(tallies), jnp.arange(rows * top), side="right").astype(jnp.int32)
    listing = labels.reshape(top, rows).T
    listing = listing[jax.random.permutation(jax.random.fold_in(own, 1), rows)]
    offset_by = jax.random.randint(jax.random.fold_in(own, 2), (rows, 1), 0, top)
    return jnp.take_along_axis(listing, (jnp.arange(top)[None, :] + offset_by) % top, axis=1)


def portions_of(number_of, total, most, skew, full):
    weights = [(1 << 20) // math.isqrt(grade ** skew) + 1 for grade in range(1, number_of + 1)]
    largest = most if full else min(most, max(-(-total // number_of), total * weights[0] // sum(weights)))
    least = 1 if total - largest >= number_of - 1 else 0
    given, spare = [largest] + [least] * (number_of - 1), total - largest - least * (number_of - 1)
    while spare > 0:
        movable = [i for i in range(1, number_of) if given[i] < largest] or [i for i in range(1, number_of) if given[i] < most]
        pool, left = sum([weights[i] for i in movable]), spare
        for i in movable:
            addition = min(most - given[i], max(1, left * weights[i] // pool), spare)
            given[i] = given[i] + addition
            spare = spare - addition
    return np.array(given)


def scatter_about(rng, dims, width, bound, split=(), held_as=jnp.bfloat16):
    gain = block_levels(rng, dims, split, -0.22, 0.18) if split else 1.0
    values = jax.random.normal(rng, dims, jnp.float32) * width * gain
    return jnp.minimum(jnp.maximum(values, -bound), bound).astype(held_as)


def heavy_noise(stream_key, extent, width, bound, pieces, heavy, kind=jnp.bfloat16):
    values = width * jax.random.normal(stream_key, extent, jnp.float32)
    if pieces:
        values = values * block_levels(stream_key, extent, pieces, -0.22, 0.18)
    return jnp.clip(spiked(values, jax.random.fold_in(stream_key, 3), *heavy), -bound, bound).astype(kind)


def setup_inputs(seed: int = 0) -> dict:
    key_list = jax.random.split(jax.random.key(seed), 18)
    tokens = scatter_about(key_list[0], (IMAGES, LEN, D), 1.0, 6.0, ((0, 32),))
    routes_keys = jax.random.split(jax.random.fold_in(key_list[1], 1), IMAGES * LEN // TOK_DEV)
    routes_turns = jax.random.permutation(jax.random.fold_in(key_list[1], 3), IMAGES * LEN // TOK_DEV)
    routes = jax.vmap(lambda own, number: deal_out(jax.random.fold_in(key_list[1], 2), own, number, TOK_DEV, EXPERTS, 2, CAP, 1))(routes_keys, routes_turns).reshape((IMAGES, LEN, 2))
    cotangent = heavy_noise(key_list[2], (IMAGES, LEN, D), 1.0, 6.0, ((0, 32),), (0, 2, 32, 2.75))
    attn_gain = jnp.clip(1.0 + 0.18 * jax.random.normal(key_list[3], (D,), jnp.float32), 0.099609375, 1.8984375).astype(jnp.bfloat16)
    attn_shift = scatter_about(key_list[4], (D,), 0.5, 3.0, ((0, 4),))
    qkv_weight = scatter_about(key_list[5], (D, 3 * D), D ** -0.5, 0.21875, ((0, 4),))
    query_bias = scatter_about(key_list[6], (D,), 0.5, 3.0, ((0, 4),))
    value_bias = scatter_about(key_list[7], (D,), 0.5, 3.0, ((0, 4),))
    proj_weight = scatter_about(key_list[8], (D, D), (D // 16) ** -0.5, 0.875, ((0, 4),))
    proj_bias = scatter_about(key_list[9], (D,), 0.5, 3.0, ((0, 4),))
    moe_gain = jnp.clip(1.0 + 0.18 * jax.random.normal(key_list[10], (D,), jnp.float32), 0.099609375, 1.8984375).astype(jnp.bfloat16)
    moe_shift = scatter_about(key_list[11], (D,), 0.5, 3.0, ((0, 4),))
    router_weight = scatter_about(key_list[12], (D, EXPERTS), D ** -0.5, 0.21875, ((0, 4),))
    expert_in = scatter_about(key_list[13], (EXPERTS, D, FF), D ** -0.5, 0.21875, ((0, 4),))
    expert_in_bias = scatter_about(key_list[14], (EXPERTS, FF), 0.5, 3.0, ((0, 4),))
    expert_out = scatter_about(key_list[15], (EXPERTS, FF, D), (max(FF // (EXPERTS * EXPERTS), 1)) ** -0.5, 0.4375, ((0, 4),))
    expert_out_bias = scatter_about(key_list[16], (EXPERTS, D), 0.5, 3.0, ((0, 4),))
    return {"tokens": tokens, "routes": routes, "cotangent": cotangent, "attn_gain": attn_gain, "attn_shift": attn_shift, "qkv_weight": qkv_weight, "query_bias": query_bias, "value_bias": value_bias, "proj_weight": proj_weight, "proj_bias": proj_bias, "moe_gain": moe_gain, "moe_shift": moe_shift, "router_weight": router_weight, "expert_in": expert_in, "expert_in_bias": expert_in_bias, "expert_out": expert_out, "expert_out_bias": expert_out_bias}


EPS = 1e-06
HIGH = lax.Precision.HIGHEST

@jax.custom_vjp
def low(v):
    return lax.optimization_barrier(v.astype(jnp.bfloat16)).astype(jnp.float32)

@jax.custom_vjp
def low_back(v):
    return v

def low_keep(v):
    return (low(v), None)

def low_pass(kept, grad):
    return (grad,)

def back_keep(v):
    return (v, None)

def back_low(kept, grad):
    return (low(grad),)
low.defvjp(low_keep, low_pass)
low_back.defvjp(back_keep, back_low)

def normalize(values_in, gain_vec, shift_vec):
    row_mean = lax.optimization_barrier(jnp.mean(values_in, axis=-1, keepdims=True))
    centered = values_in - row_mean
    variance = lax.optimization_barrier(jnp.mean(centered * centered, axis=-1, keepdims=True))
    return centered * lax.rsqrt(variance + EPS) * gain_vec + shift_vec

def attend(packed):
    group_size = packed.shape[0]
    query_rows = packed[..., :D].reshape(group_size, LEN, HEADS, HEAD_DIM)
    key_rows = packed[..., D:2 * D].reshape(group_size, LEN, HEADS, HEAD_DIM)
    value_rows = packed[..., 2 * D:].reshape(group_size, LEN, HEADS, HEAD_DIM)
    scores = low_back(jnp.einsum('glhd,gmhd->ghlm', query_rows, key_rows, precision=HIGH) * HEAD_DIM ** (-0.5))
    weights = low(jax.nn.softmax(scores, axis=-1))
    mixed_rows = jnp.einsum('ghlm,gmhd->glhd', weights, value_rows, precision=HIGH)
    return mixed_rows.reshape(group_size, LEN, D)

def forward(tokens_in, params, route_ids):
    attn_gain, attn_shift, qkv_weight, query_bias, value_bias, proj_weight, proj_bias, moe_gain, moe_shift, router_weight, expert_in, expert_in_bias, expert_out, expert_out_bias = params
    first_norm = low(normalize(tokens_in, attn_gain, attn_shift))
    qkv_bias = jnp.concatenate([query_bias, jnp.zeros_like(query_bias), value_bias])
    projected = low_back(low(jnp.einsum('ild,de->ile', first_norm, qkv_weight, precision=HIGH) + qkv_bias))
    grouped = projected.reshape(IMAGES // 16, 16, LEN, 3 * D)
    attended = lax.map(jax.checkpoint(attend), grouped).reshape(IMAGES, LEN, D)
    attended = low_back(low(attended))
    branch = low_back(jnp.einsum('ild,de->ile', attended, proj_weight, precision=HIGH) + proj_bias)
    middle = tokens_in + branch
    second = low(normalize(middle, moe_gain, moe_shift)).reshape(IMAGES * LEN, D)
    logits = low_back(jnp.dot(second, router_weight, precision=HIGH))
    router_probs = jax.nn.softmax(logits, axis=-1)
    pair_ids = route_ids.reshape(IMAGES * LEN, 2)
    gate_pair = jnp.take_along_axis(router_probs, pair_ids, axis=1)
    flat_ids = pair_ids.reshape(IMAGES * LEN * 2)
    copies = low_back(jnp.repeat(second, 2, axis=0))

    def one_expert(summed, packed):
        index, w_first, b_first, w_second, b_second = packed
        pre_act = low_back(jnp.dot(copies, w_first, precision=HIGH) + b_first)
        hidden = low(jax.nn.gelu(pre_act, approximate=True))
        result = low_back(low(jnp.dot(hidden, w_second, precision=HIGH) + b_second))
        chosen = (flat_ids == index).astype(jnp.float32)[:, None]
        return (summed + chosen * result, None)
    start = jnp.zeros((IMAGES * LEN * 2, D), jnp.float32)
    summed, _ = lax.scan(jax.checkpoint(one_expert), start, (jnp.arange(EXPERTS, dtype=jnp.int32), expert_in, expert_in_bias, expert_out, expert_out_bias))
    combined = lax.optimization_barrier(jnp.sum(gate_pair[:, :, None] * summed.reshape(IMAGES * LEN, 2, D), axis=1))
    return middle + combined.reshape(IMAGES, LEN, D)

def reference(tokens, routes, cotangent, attn_gain, attn_shift, qkv_weight, query_bias, value_bias, proj_weight, proj_bias, moe_gain, moe_shift, router_weight, expert_in, expert_in_bias, expert_out, expert_out_bias):
    params = tuple((item.astype(jnp.float32) for item in (attn_gain, attn_shift, qkv_weight, query_bias, value_bias, proj_weight, proj_bias, moe_gain, moe_shift, router_weight, expert_in, expert_in_bias, expert_out, expert_out_bias)))

    def whole_block(tokens_in, weights):
        return forward(tokens_in, weights, routes)
    result, pullback = jax.vjp(whole_block, tokens.astype(jnp.float32), params)
    token_grad, weight_grads = pullback(cotangent.astype(jnp.float32))
    return (result.astype(jnp.bfloat16), token_grad, weight_grads[0], weight_grads[1], weight_grads[2], weight_grads[3], weight_grads[4], weight_grads[5], weight_grads[6], weight_grads[7], weight_grads[8], weight_grads[9], weight_grads[10], weight_grads[11], weight_grads[12], weight_grads[13])
```

```python
from functools import partial

import jax
import jax.numpy as jnp
from jax import lax
from jax.sharding import PartitionSpec as P

HEADS = 12
HEAD_DIM = 64


EPS = 1e-06


def normalize(values_in, gain_vec, shift_vec):
    row_mean = jnp.mean(values_in, axis=-1, keepdims=True)
    centered = values_in - row_mean
    inverse = lax.rsqrt(jnp.mean(centered * centered, axis=-1, keepdims=True) + EPS)
    normed = centered * inverse
    return (normed * gain_vec + shift_vec, normed, inverse)


def normalize_back(incoming, normed, inverse, gain_vec):
    scaled = incoming * gain_vec
    inner_mean = jnp.mean(scaled, axis=-1, keepdims=True)
    cross_mean = jnp.mean(scaled * normed, axis=-1, keepdims=True)
    back = inverse * (scaled - inner_mean - normed * cross_mean)
    return (back, jnp.sum(incoming * normed, axis=0), jnp.sum(incoming, axis=0))


def split_heads(block, image_count, seq_length):
    return block.reshape(image_count, seq_length, HEADS, HEAD_DIM)


def gather_params(packed):
    share = packed.shape[0] // lax.axis_size("rep")
    mine = lax.dynamic_slice_in_dim(packed, lax.axis_index("rep") * share, share, 0)
    across = lax.all_gather(mine, "exp", axis=0, tiled=False)
    return lax.all_gather(across, "rep", axis=1, tiled=False).reshape(-1, packed.shape[1])


def local(
    tokens,
    routes,
    cotangent,
    attn_gain,
    attn_shift,
    qkv_weight,
    query_bias,
    value_bias,
    proj_weight,
    proj_bias,
    moe_gain,
    moe_shift,
    router_weight,
    expert_in,
    expert_in_bias,
    expert_out,
    expert_out_bias,
):
    image_count, seq_length, model_width = tokens.shape
    row_count = image_count * seq_length
    expert_count = lax.axis_size("exp")
    capacity = min(row_count, (row_count * 8 // (3 * expert_count) + 7) // 8 * 8)
    score_scale = HEAD_DIM ** (-0.5)
    own = lax.axis_index("exp")
    low = jnp.bfloat16
    wide = jnp.float32
    pair = routes.reshape(row_count, 2)
    expert_ids = jnp.arange(expert_count, dtype=jnp.int32)
    named = pair[:, :, None] == expert_ids[None, None, :]
    member = jnp.sum(named.astype(jnp.int32), axis=1)
    earlier = (
        jnp.arange(row_count)[:, None] > jnp.arange(row_count)[None, :]
    ).astype(low)
    slots = jnp.dot(earlier, member.astype(low), preferred_element_type=wide).astype(jnp.int32)
    place = jnp.sum(
        named * (slots + expert_ids[None, :] * capacity)[:, None, :], axis=2
    )
    slot_total = expert_count * capacity
    all_slots = jnp.arange(slot_total, dtype=jnp.int32)
    chosen = named.astype(wide)
    pick_0 = (place[:, 0][:, None] == all_slots[None, :]).astype(low)
    pick_1 = (place[:, 1][:, None] == all_slots[None, :]).astype(low)
    pick_both = pick_0 + pick_1

    def send_out(rows):
        filled = lax.dot_general(
            pick_both, rows, (((0,), (0,)), ((), ())), preferred_element_type=wide
        ).astype(low)
        return exchange(filled)

    def exchange(filled):
        return lax.all_to_all(
            filled.reshape(expert_count, capacity, model_width),
            "exp",
            split_axis=0,
            concat_axis=0,
            tiled=True,
        ).reshape(slot_total, model_width)

    vector_width = 128
    columns = jnp.concatenate(
        [
            jnp.stack(
                [
                    attn_gain,
                    attn_shift,
                    query_bias,
                    value_bias,
                    proj_bias,
                    moe_gain,
                    moe_shift,
                ],
                axis=1,
            ),
            router_weight,
        ],
        axis=1,
    )
    columns = jnp.pad(columns, ((0, 0), (0, vector_width - columns.shape[1])))
    packed = jnp.concatenate([qkv_weight, proj_weight, columns], axis=1)
    full = gather_params(packed)
    qkv_full = full[:, : 3 * model_width]
    proj_full = full[:, 3 * model_width : 4 * model_width]
    vectors = full[:, 4 * model_width :]
    router_full = vectors[:, 7 : 7 + expert_count]
    vector_rows = vectors[:, :7].T.astype(wide)
    gain_one = vector_rows[0]
    shift_one = vector_rows[1]
    query_add = vector_rows[2]
    value_add = vector_rows[3]
    proj_add = vector_rows[4]
    gain_two = vector_rows[5]
    shift_two = vector_rows[6]

    cotangent_rows = cotangent.reshape(row_count, model_width)
    slot_cotangent = send_out(cotangent_rows)

    source = tokens.reshape(row_count, model_width).astype(wide)
    first_out, normed_one, inverse_one = normalize(source, gain_one, shift_one)
    first_low = first_out.astype(low)
    qkv_bias = jnp.concatenate([query_add, jnp.zeros_like(query_add), value_add])
    qkv_low = (jnp.dot(first_low, qkv_full, preferred_element_type=wide) + qkv_bias).astype(low)
    query_rows = split_heads(qkv_low[:, :model_width], image_count, seq_length)
    key_rows = split_heads(qkv_low[:, model_width : 2 * model_width], image_count, seq_length)
    value_rows = split_heads(qkv_low[:, 2 * model_width :], image_count, seq_length)
    scores = (
        jnp.einsum("ilhd,imhd->ihlm", query_rows, key_rows, preferred_element_type=wide)
        * score_scale
    )
    score_top = jnp.max(scores, axis=-1, keepdims=True)
    log_total = score_top + jnp.log(jnp.sum(jnp.exp(scores - score_top), axis=-1, keepdims=True))
    attn_probs = jnp.exp(scores - log_total)
    attended = (
        jnp.einsum(
            "ihlm,imhd->ilhd", attn_probs.astype(low), value_rows, preferred_element_type=wide
        )
        .reshape(row_count, model_width)
        .astype(low)
    )
    branch = jnp.dot(attended, proj_full, preferred_element_type=wide) + proj_add
    middle = source + branch
    second_out, normed_two, inverse_two = normalize(middle, gain_two, shift_two)
    second_low = second_out.astype(low)
    expert_rows = send_out(second_low)

    logits = jnp.dot(second_low, router_full, preferred_element_type=wide)
    router_probs = jax.nn.softmax(logits, axis=-1)
    gates = jnp.sum(chosen * router_probs[:, None, :], axis=2)

    slot_probs = jax.nn.softmax(
        jnp.dot(expert_rows, router_full, preferred_element_type=wide), axis=-1
    )
    slot_gates = jnp.sum(
        jnp.where(expert_ids[None, :] == own, slot_probs, 0.0), axis=1, keepdims=True
    )
    result_grad = (slot_gates * slot_cotangent.astype(wide)).astype(low)
    pre_act = jnp.dot(expert_rows, expert_in[0], preferred_element_type=wide) + expert_in_bias[
        0
    ].astype(wide)
    hidden_low = jax.nn.gelu(pre_act, approximate=True).astype(low)
    result = (
        jnp.dot(hidden_low, expert_out[0], preferred_element_type=wide)
        + expert_out_bias[0].astype(wide)
    ).astype(low)
    returned = exchange(result)
    hidden_grad = jnp.einsum("rd,fd->rf", result_grad, expert_out[0], preferred_element_type=wide)
    _, gelu_back = jax.vjp(partial(jax.nn.gelu, approximate=True), pre_act)
    pre_grad = gelu_back(hidden_grad)[0].astype(low)
    row_back = jnp.einsum("rf,df->rd", pre_grad, expert_in[0], preferred_element_type=wide).astype(
        low
    )
    came_back = exchange(row_back)
    grad_w_down = jnp.einsum(
        "rf,rd->fd", hidden_low, result_grad, preferred_element_type=wide
    ).astype(low)
    grad_down_bias = jnp.sum(result_grad.astype(wide), axis=0)
    grad_w_first = jnp.einsum(
        "rd,rf->df", expert_rows, pre_grad, preferred_element_type=wide
    ).astype(low)
    grad_first_bias = jnp.sum(pre_grad.astype(wide), axis=0)
    grad_w_first, grad_w_down = lax.psum((grad_w_first, grad_w_down), "rep")

    picked_0 = jnp.dot(pick_0, returned, preferred_element_type=wide)
    picked_1 = jnp.dot(pick_1, returned, preferred_element_type=wide)
    output = middle + gates[:, 0:1] * picked_0 + gates[:, 1:2] * picked_1
    block_out = output.reshape(image_count, seq_length, model_width).astype(low)
    out_grad = cotangent_rows.astype(wide)
    gate_grad_0 = jnp.sum(out_grad * picked_0, axis=1, keepdims=True)
    gate_grad_1 = jnp.sum(out_grad * picked_1, axis=1, keepdims=True)
    prob_grad = chosen[:, 0] * gate_grad_0 + chosen[:, 1] * gate_grad_1
    logit_grad = router_probs * (
        prob_grad - jnp.sum(prob_grad * router_probs, axis=-1, keepdims=True)
    )
    logit_low = logit_grad.astype(low)
    grad_router = jnp.einsum("rd,re->de", second_low, logit_low, preferred_element_type=wide)
    norm_grad = jnp.dot(pick_both, came_back, preferred_element_type=wide) + jnp.einsum(
        "re,de->rd", logit_low, router_full, preferred_element_type=wide
    )
    middle_part, grad_gain_two, grad_shift_two = normalize_back(
        norm_grad, normed_two, inverse_two, gain_two
    )
    middle_grad = out_grad + middle_part
    branch_low = middle_grad.astype(low)
    grad_proj = jnp.einsum("rd,re->de", attended, branch_low, preferred_element_type=wide)
    grad_proj_bias = jnp.sum(branch_low.astype(wide), axis=0)
    attended_grad = split_heads(
        jnp.einsum("re,de->rd", branch_low, proj_full, preferred_element_type=wide).astype(low),
        image_count,
        seq_length,
    )
    weight_grad = jnp.einsum(
        "ilhd,imhd->ihlm", attended_grad, value_rows, preferred_element_type=wide
    )
    value_grad = jnp.einsum(
        "ihlm,ilhd->imhd", attn_probs.astype(low), attended_grad, preferred_element_type=wide
    )
    score_grad = (
        attn_probs * (weight_grad - jnp.sum(weight_grad * attn_probs, axis=-1, keepdims=True))
    ).astype(low)
    query_grad = (
        jnp.einsum("ihlm,imhd->ilhd", score_grad, key_rows, preferred_element_type=wide)
        * score_scale
    )
    key_grad = (
        jnp.einsum("ihlm,ilhd->imhd", score_grad, query_rows, preferred_element_type=wide)
        * score_scale
    )
    qkv_grad = jnp.concatenate(
        [
            query_grad.reshape(row_count, model_width),
            key_grad.reshape(row_count, model_width),
            value_grad.reshape(row_count, model_width),
        ],
        axis=1,
    ).astype(low)
    grad_qkv = jnp.einsum("rd,re->de", first_low, qkv_grad, preferred_element_type=wide)
    qkv_sums = jnp.sum(qkv_grad.astype(wide), axis=0)
    first_grad = jnp.einsum("re,de->rd", qkv_grad, qkv_full, preferred_element_type=wide)
    source_part, grad_gain_one, grad_shift_one = normalize_back(
        first_grad, normed_one, inverse_one, gain_one
    )
    input_grad = (middle_grad + source_part).reshape(image_count, seq_length, model_width)

    owned_rows = model_width // expert_count
    bias_columns = (grad_first_bias.shape[0] + model_width) // owned_rows
    own_bias = jnp.concatenate([grad_first_bias, grad_down_bias]).reshape(bias_columns, owned_rows)
    own_bias = jnp.tile(own_bias.T, (expert_count, 1))
    is_own = (jnp.arange(model_width) // owned_rows == own)[:, None]
    vector_grads = jnp.concatenate(
        [
            jnp.stack(
                [
                    grad_gain_one,
                    grad_shift_one,
                    qkv_sums[:model_width],
                    qkv_sums[2 * model_width :],
                    grad_proj_bias,
                    grad_gain_two,
                    grad_shift_two,
                ],
                axis=1,
            ),
            grad_router,
            jnp.where(is_own, own_bias, 0.0),
        ],
        axis=1,
    )
    vector_grads = jnp.pad(vector_grads, ((0, 0), (0, vector_width - vector_grads.shape[1])))
    dense_packed = jnp.concatenate([grad_qkv, grad_proj, vector_grads], axis=1).astype(low)
    dense_owned = lax.psum_scatter(dense_packed, "exp", scatter_dimension=0, tiled=True)
    dense_owned, grad_w_first, grad_w_down = lax.optimization_barrier(
        (dense_owned, grad_w_first, grad_w_down)
    )
    dense_summed = lax.psum(dense_owned, "rep").astype(wide)
    summed_vectors = dense_summed[:, 4 * model_width :]
    summed_rows = summed_vectors.T
    router_end = 7 + expert_count
    summed_bias = summed_rows[router_end : router_end + bias_columns].reshape(
        1, bias_columns * owned_rows
    )
    first_width = grad_first_bias.shape[0]
    return (
        block_out,
        input_grad,
        summed_rows[0],
        summed_rows[1],
        dense_summed[:, : 3 * model_width],
        summed_rows[2],
        summed_rows[3],
        dense_summed[:, 3 * model_width : 4 * model_width],
        summed_rows[4],
        summed_rows[5],
        summed_rows[6],
        summed_vectors[:, 7:router_end],
        grad_w_first.astype(wide)[None],
        summed_bias[:, :first_width],
        grad_w_down.astype(wide)[None],
        summed_bias[:, first_width:],
    )


def solution(mesh):
    return jax.shard_map(
        local,
        mesh=mesh,
        in_specs=(
            P(("rep", "exp"), None, None),
            P(("rep", "exp"), None, None),
            P(("rep", "exp"), None, None),
            P("exp"),
            P("exp"),
            P("exp", None),
            P("exp"),
            P("exp"),
            P("exp", None),
            P("exp"),
            P("exp"),
            P("exp"),
            P("exp", None),
            P("exp", None, None),
            P("exp", None),
            P("exp", None, None),
            P("exp", None),
        ),
        out_specs=(
            P(("rep", "exp"), None, None),
            P(("rep", "exp"), None, None),
            P("exp"),
            P("exp"),
            P("exp", None),
            P("exp"),
            P("exp"),
            P("exp", None),
            P("exp"),
            P("exp"),
            P("exp"),
            P("exp", None),
            P("exp", None, None),
            P("exp", None),
            P("exp", None, None),
            P("exp", None),
        ),
        check_vma=False,
    )
```
